32 devices in a mesh: rows: 4 (over z), cols: 4 (over y, x), slab: 2 (over core).
Axes of the slice: x: 2, y: 2, z: 4, core: 2. Of those that a mesh axis runs over, the one named last changes fastest.
Arguments:
- density_blocks: bfloat16 [2048, 4096], P(('rows', 'cols', 'slab')), may hold values from -6 to 6
- block_owner: int32 [2048, 1], P(('rows', 'cols', 'slab')), may hold values from 0 to 31; in each aligned block of 64 rows (0 to 63, 64 to 127, ...) at most 4 rows name the same one
- block_plane: int32 [2048], P(('rows', 'cols', 'slab')), may hold values from 0 to 7
- block_segment: int32 [2048], P(('rows', 'cols', 'slab')), may hold values from 0 to 7
- block_kinds: int32 [2048, 2], P(('rows', 'cols', 'slab')), may hold values from 0 to 3
- basis: bfloat16 [4, 64, 4096], replicated, may hold values from -1.015625 to 1.015625
- ext_potential: float32 [256, 4096], P(('rows', 'cols', 'slab')), may hold values from -6 to 6
Outputs:
- density: float32 [256, 4096], P(('rows', 'cols', 'slab'))
- matrix_blocks: bfloat16 [2048, 4096], P(('rows', 'cols', 'slab'))
The draws below stay inside these ranges and needn't reach their ends.
Inputs may be any that keep to these rules, and one draw needn't show every extreme that they name: `block_owner`: among the blocks of one device no owner is named more than 4 times; some owner is named exactly 4 times.
All inputs are finite; a program needn't handle non-finite values.
Results may differ from the reference program's by a relative error of at most 0.0095.
Values may be sent and summed in bfloat16 or wider, within the bound.
A program may use at most 128 MiB of HBM per device.

```python
import math
import jax
import jax.numpy as jnp
import numpy as np
from jax import lax

BS = 64
KINDS = 4
CZB = 8
SEGW = 512
NB_DEV = 64
ZDEV = 8
PLANE = 4096
CUBE = 4096
SEGS = 8
CAP = 4
NBLOCKS = 2048
NZ = 256
DEVICES = 32


def plant(array, stream_key, least, high):
    longest = array.shape.index(max(array.shape))
    spots = []
    for shift in (0, 1):
        where = [jax.random.randint(jax.random.fold_in(stream_key, axis), (), 0, length) for axis, length in enumerate(array.shape)]
        where[longest] = (where[longest] + shift) % array.shape[longest]
        spots.append(tuple(where))
    return array.at[spots[0]].set(least).at[spots[1]].set(high)


def steps_of(own_key, shape, shards, smallest, largest):
    def one(axis_at, parts):
        steps = jax.random.uniform(jax.random.fold_in(jax.random.fold_in(own_key, 6), axis_at), (parts,), jnp.float32, smallest / len(shards), largest / len(shards))
        return jnp.repeat(jnp.exp(steps), shape[axis_at] // parts).reshape((-1,) + (1,) * (len(shape) - axis_at - 1))

    gain = one(*shards[0])
    for cut in shards[1:]:
        gain = gain * one(*cut)
    return gain


def routed_block(rng, own, number, rows, amount, top, bound, slope):
    sequence = jax.random.permutation(rng, amount)
    crowded, ordinary = load_shares(amount, rows * top, bound, slope, True), load_shares(amount, rows * top, bound, slope, False)
    places = jnp.arange(amount)

    def named(tallies, turn):
        used = int((tallies > 0).sum())
        fixed = max(1, used // 4)
        moved = fixed + (places - fixed + turn * (used - fixed)) % max(1, amount - fixed)
        return jnp.zeros((amount,), jnp.int32).at[sequence[jnp.where(places < fixed, places, moved)]].set(jnp.asarray(tallies, jnp.int32))

    tallies = jnp.where(number % 4 == 0, named(crowded, number // 4), named(ordinary, number - number // 4 - 1))
    mixed = jax.random.permutation(jax.random.fold_in(own, 3), amount)
    donor, sink = mixed[0:amount // 2 * 2:2], mixed[1:amount // 2 * 2:2]
    margin = jnp.minimum(tallies[donor] - 1, bound - tallies[sink]) // 2
    margin = jnp.where((donor == sequence[0]) | (sink == sequence[0]) | (tallies[sink] == 0), 0, jnp.maximum(margin, 0))
    moved = jax.random.randint(jax.random.fold_in(own, 4), (amount // 2,), 0, 1 << 20) % (margin + 1)
    tallies = tallies.at[donor].add(-moved).at[sink].add(moved)
    members = jnp.searchsorted(jnp.cumsum(tallies), jnp.arange(rows * top), side="right").astype(jnp.int32)
    table = members.reshape(top, rows).T
    table = table[jax.random.permutation(jax.random.fold_in(own, 1), rows)]
    turn = jax.random.randint(jax.random.fold_in(own, 2), (rows, 1), 0, top)
    return jnp.take_along_axis(table, (jnp.arange(top)[None, :] + turn) % top, axis=1)


def load_shares(amount, total, most, slope, full):
    weights = [(1 << 20) // math.isqrt(rank ** slope) + 1 for rank in range(1, amount + 1)]
    largest = most if full else min(most, max(-(-total // amount), total * weights[0] // sum(weights)))
    least = 1 if total - largest >= amount - 1 else 0
    given, surplus = [largest] + [least] * (amount - 1), total - largest - least * (amount - 1)
    while surplus > 0:
        free = [i for i in range(1, amount) if given[i] < largest] or [i for i in range(1, amount) if given[i] < most]
        pool, budget = sum([weights[i] for i in free]), surplus
        for i in free:
            more = min(most - given[i], max(1, budget * weights[i] // pool), surplus)
            given[i] = given[i] + more
            surplus = surplus - more
    return np.array(given)


def gaussian(key, extent, width, reach, pieces=(), kind=jnp.bfloat16):
    entries = jax.random.normal(key, extent, jnp.float32) * width
    if len(pieces) > 0:
        entries = steps_of(key, extent, pieces, -0.22, 0.18) * entries
    return jnp.clip(entries, min=-reach, max=reach).astype(kind)


def setup_inputs(seed: int = 0) -> dict:
    streams_of = jax.random.split(jax.random.key(seed), 8)
    density_blocks = gaussian(streams_of[0], (NBLOCKS, BS * BS), 1.0, 6.0, ((0, 32),))
    block_owner_keys = jax.random.split(jax.random.fold_in(streams_of[1], 1), NBLOCKS // NB_DEV)
    block_owner_turns = jax.random.permutation(jax.random.fold_in(streams_of[1], 3), NBLOCKS // NB_DEV)
    block_owner = jax.vmap(lambda own, number: routed_block(jax.random.fold_in(streams_of[1], 2), own, number, NB_DEV, DEVICES, 1, CAP, 2))(block_owner_keys, block_owner_turns).reshape((NBLOCKS, 1))
    block_plane = plant(jax.random.randint(streams_of[2], (NBLOCKS,), 0, ZDEV), jax.random.fold_in(streams_of[2], 1), 0, ZDEV - 1).astype(jnp.int32)
    block_segment = plant(jax.random.randint(streams_of[3], (NBLOCKS,), 0, SEGS), jax.random.fold_in(streams_of[3], 1), 0, SEGS - 1).astype(jnp.int32)
    block_kinds = plant(jax.random.randint(streams_of[4], (NBLOCKS, 2), 0, KINDS), jax.random.fold_in(streams_of[4], 1), 0, KINDS - 1).astype(jnp.int32)
    basis = gaussian(streams_of[5], (KINDS, BS, CUBE), (1.36 / BS ** 0.5), 1.015625)
    ext_potential = gaussian(streams_of[6], (NZ, PLANE), 1.0, 6.0, ((0, 32),), jnp.float32)
    return dict(density_blocks=density_blocks, block_owner=block_owner, block_plane=block_plane, block_segment=block_segment, block_kinds=block_kinds, basis=basis, ext_potential=ext_potential)


def reference(density_blocks, block_owner, block_plane, block_segment, block_kinds, basis, ext_potential):
    segs = PLANE // SEGW
    rows_total = NZ * segs
    per_batch = 64
    batch_count = density_blocks.shape[0] // per_batch
    start_plane = (block_owner[:, 0] * ZDEV + block_plane).astype(jnp.int32)
    offsets = jnp.arange(CZB, dtype=jnp.int32)
    row_index = (((start_plane[:, None] + offsets[None, :]) % NZ) * segs + block_segment[:, None]).astype(jnp.int32)
    row_batches = row_index.reshape(batch_count, per_batch, CZB)
    kind_batches = block_kinds.reshape(batch_count, per_batch, 2)
    block_batches = density_blocks.reshape(batch_count, per_batch, BS, BS)

    def deposit(grid_rows, batch_item):
        block_batch, index_batch, kind_pair = batch_item
        row_basis = basis[kind_pair[:, 0]].astype(jnp.float32)
        col_basis = basis[kind_pair[:, 1]].astype(jnp.float32)
        half_product = jnp.einsum("bmn,bnc->bmc", block_batch.astype(jnp.float32), col_basis).astype(jnp.bfloat16)
        half_product = lax.optimization_barrier(half_product).astype(jnp.float32)
        product_tile = jnp.sum(row_basis * half_product, axis=1)
        added = jax.ops.segment_sum(product_tile.reshape(-1, SEGW), index_batch.reshape(-1), num_segments=rows_total)
        return grid_rows + added, None

    grid_rows, _ = lax.scan(deposit, jnp.zeros((rows_total, SEGW), jnp.float32), (block_batches, row_batches, kind_batches))
    density = grid_rows.reshape(NZ, PLANE)
    potential = (ext_potential + 0.5 * density).reshape(rows_total, SEGW)

    def integrate(carry, batch_item):
        index_batch, kind_pair = batch_item
        row_basis = basis[kind_pair[:, 0]].astype(jnp.float32)
        col_basis = basis[kind_pair[:, 1]].astype(jnp.float32)
        pot_tile = potential[index_batch.reshape(-1)].reshape(per_batch, CUBE)
        weighted = (row_basis * pot_tile[:, None, :]).astype(jnp.bfloat16)
        weighted = lax.optimization_barrier(weighted).astype(jnp.float32)
        matrix_tile = jnp.einsum("bmc,bnc->bmn", weighted, col_basis).astype(jnp.bfloat16)
        return carry, matrix_tile.reshape(per_batch, BS * BS)

    _, matrix_tiles = lax.scan(integrate, jnp.zeros((), jnp.float32), (row_batches, kind_batches))
    return density, matrix_tiles.reshape(NBLOCKS, BS * BS)
```

```python
import functools

import jax
import jax.numpy as jnp
from jax import lax
from jax.experimental import pallas as pl
from jax.experimental.pallas import tpu as pltpu
from jax.sharding import PartitionSpec as P

CZB = 8
SEGW = 512
TILE = 256
AXES = ("rows", "cols", "slab")
VMEM = pl.BlockSpec(memory_space=pltpu.VMEM)
MESH = pl.DeviceIdType.MESH
SMEM = pl.BlockSpec(memory_space=pltpu.SMEM)


def deposit_kernel(width, count, kinds_ref, rows_ref, wide_ref, basis_ref, grid_ref, tiles_ref):
    halves = SEGW // TILE
    group = 8
    cells = basis_ref.shape[1]

    def column_tile(t, carry):
        i, h = t // halves, t % halves
        columns = pl.ds(pl.multiple_of(t * TILE, TILE), TILE)
        weights = basis_ref[:, columns]
        for g in range(count // group):
            lhs = wide_ref[pl.ds(g * group * width, group * width), :]
            half = jnp.dot(lhs, weights, preferred_element_type=jnp.float32)
            sums = []
            for b in range(group):
                kind = kinds_ref[g * group + b, 0]
                a = basis_ref[pl.ds(pl.multiple_of(kind * width, width), width), columns]
                product = a.astype(jnp.float32) * half[b * width : (b + 1) * width]
                sums.append(jnp.sum(product, axis=0, keepdims=True))
            row = pl.multiple_of(i * count + g * group, group)
            tiles_ref[pl.ds(row, group), pl.ds(pl.multiple_of(h * TILE, TILE), TILE)] = (
                jnp.concatenate(sums, axis=0)
            )
        return carry

    lax.fori_loop(0, cells // TILE, column_tile, 0)
    tiles = tiles_ref[...].astype(jnp.bfloat16)
    places = tiles.shape[0]
    chunk = 256

    def place(r, carry):
        base = pl.multiple_of(r * chunk, chunk)
        hot = rows_ref[...] == lax.broadcasted_iota(jnp.int32, (chunk, places), 0) + base
        hot = jnp.where(hot, 1.0, 0.0).astype(jnp.bfloat16)
        placed = jnp.dot(hot, tiles, preferred_element_type=jnp.float32).astype(jnp.bfloat16)
        for h in range(SEGW // TILE):
            grid_ref[h, pl.ds(base, chunk), :] = placed[:, h * TILE : (h + 1) * TILE]
        return carry

    lax.fori_loop(0, grid_ref.shape[1] // chunk, place, 0)


def integrate_kernel(
    width, count, kinds_ref, rows_ref, pot_ref, basis_ref, out_ref, tiles_ref, weighted_ref
):
    halves = SEGW // TILE
    group = 8
    cells = basis_ref.shape[1]
    places = tiles_ref.shape[0]
    grid_rows = pot_ref.shape[1]
    chunk = 256

    tiles_ref[...] = jnp.zeros_like(tiles_ref)

    def gather(r, carry):
        base = pl.multiple_of(r * chunk, chunk)
        hot = rows_ref[...] == lax.broadcasted_iota(jnp.int32, (places, chunk), 1) + base
        hot = jnp.where(hot, 1.0, 0.0).astype(jnp.bfloat16)
        for h in range(halves):
            tiles_ref[:, pl.ds(h * TILE, TILE)] += jnp.dot(
                hot, pot_ref[h, pl.ds(base, chunk), :], preferred_element_type=jnp.float32
            )
        return carry

    lax.fori_loop(0, grid_rows // chunk, gather, 0)

    def block_group(g, carry):
        for t in range(cells // TILE):
            i, h = t // halves, t % halves
            rows = pl.ds(pl.multiple_of(i * count + g * group, group), group)
            pots = tiles_ref[rows, pl.ds(h * TILE, TILE)]
            for b in range(group):
                kind = kinds_ref[g * group + b, 0]
                a = basis_ref[
                    pl.ds(pl.multiple_of(kind * width, width), width), pl.ds(t * TILE, TILE)
                ]
                weighted_ref[b * width : (b + 1) * width, t * TILE : (t + 1) * TILE] = (
                    a * jnp.broadcast_to(pots[b : b + 1], (width, TILE)).astype(jnp.bfloat16)
                )
        full = lax.dot_general(
            weighted_ref[...],
            basis_ref[...],
            (((1,), (1,)), ((), ())),
            preferred_element_type=jnp.float32,
        )
        for b in range(group):
            kind = kinds_ref[g * group + b, 1]
            mine = full[b * width : (b + 1) * width]
            picked = mine[:, :width]
            for k in range(1, basis_ref.shape[0] // width):
                picked = jnp.where(kind == k, mine[:, k * width : (k + 1) * width], picked)
            out_ref[pl.ds(pl.multiple_of((g * group + b) * width, width), width), :] = (
                picked.astype(jnp.bfloat16)
            )
        return carry

    lax.fori_loop(0, count // group, block_group, 0)


def peers_of(axis):
    size = lax.axis_size(axis)
    me = lax.axis_index(axis)
    return [lax.rem(me + o, size) for o in range(1, size)]


def greet():
    barrier = pltpu.get_barrier_semaphore()
    total = 0
    for axis in AXES:
        for peer in peers_of(axis):
            pl.semaphore_signal(barrier, inc=1, device_id={axis: peer}, device_id_type=MESH)
            total += 1
    pl.semaphore_wait(barrier, total)


def send(axis, peer, src, dst, sems, at):
    copy = pltpu.make_async_remote_copy(
        src_ref=src,
        dst_ref=dst,
        send_sem=sems.at[0, at],
        recv_sem=sems.at[1, at],
        device_id={axis: peer},
        device_id_type=MESH,
    )
    copy.start()
    return copy


class Exchange:
    def __init__(self, order, grid, pots, bufs, sems):
        self.order, self.grid, self.pots, self.sems = order, grid, pots, sems
        self.got1, self.sum1, self.got2, self.sum2, self.got3 = bufs
        self.r, self.c, self.s = (lax.axis_index(axis) for axis in AXES)
        self.sizes = {axis: lax.axis_size(axis) for axis in AXES}
        self.used = 0

    def next_sem(self):
        self.used += 1
        return self.used - 1

    def start1(self):
        (peer,) = peers_of("slab")
        self.copies = [
            send("slab", peer, self.grid.at[:, :, peer], self.got1, self.sems, self.next_sem())
        ]

    def wait(self):
        for copy in self.copies:
            copy.wait()

    def start2(self):
        self.wait()
        nr, nc = self.sizes["rows"], self.sizes["cols"]

        def add(n, carry):
            r, c = n // nc, n % nc
            self.sum1[r, c] = (
                self.grid[r, c, self.s].astype(jnp.float32) + self.got1[r, c].astype(jnp.float32)
            ).astype(jnp.bfloat16)
            return carry

        lax.fori_loop(0, nr * nc, add, 0)
        axis = self.order[0]
        self.copies = []
        for o, peer in enumerate(peers_of(axis)):
            src = self.sum1.at[peer] if axis == "rows" else self.sum1.at[:, peer]
            self.copies.append(send(axis, peer, src, self.got2.at[o], self.sems, self.next_sem()))

    def start3(self):
        self.wait()
        first, axis = self.order

        def add(n, carry):
            mine = self.sum1[self.r, n] if first == "rows" else self.sum1[n, self.c]
            total = mine.astype(jnp.float32)
            for o in range(self.sizes[first] - 1):
                total = total + self.got2[o, n].astype(jnp.float32)
            self.sum2[n] = total.astype(jnp.bfloat16)
            return carry

        lax.fori_loop(0, self.sizes[axis], add, 0)
        self.copies = []
        for o, peer in enumerate(peers_of(axis)):
            self.copies.append(
                send(axis, peer, self.sum2.at[peer], self.got3.at[o], self.sems, self.next_sem())
            )

    def finish(self):
        self.wait()
        axis = self.order[1]
        total = self.sum2[self.r if axis == "rows" else self.c].astype(jnp.float32)
        for o in range(self.sizes[axis] - 1):
            total = total + self.got3[o].astype(jnp.float32)
        return total

    def start4(self, potential):
        self.pots[self.r, self.c, self.s] = potential.astype(jnp.bfloat16)
        axis = self.order[1]
        mine = self.pots.at[self.r, self.c, self.s]
        self.copies = [
            send(axis, peer, mine, mine, self.sems, self.next_sem()) for peer in peers_of(axis)
        ]

    def start5(self):
        self.wait()
        axis = self.order[0]
        if axis == "rows":
            mine = self.pots.at[self.r, :, self.s]
        else:
            mine = self.pots.at[:, self.c, self.s]
        self.copies = [
            send(axis, peer, mine, mine, self.sems, self.next_sem()) for peer in peers_of(axis)
        ]

    def start6(self):
        self.wait()
        (peer,) = peers_of("slab")
        mine = self.pots.at[:, :, self.s]
        self.copies = [send("slab", peer, mine, mine, self.sems, self.next_sem())]


ORDERS = (("cols", "rows"), ("rows", "cols"))


def exchange_scratch(nr, nc, ns, own):
    kinds = []
    for order in ORDERS:
        first, second = (nr, nc) if order[0] == "rows" else (nc, nr)
        kinds += [
            pltpu.VMEM((nr, nc, own, TILE), jnp.bfloat16),
            pltpu.VMEM((nr, nc, own, TILE), jnp.bfloat16),
            pltpu.VMEM((first - 1, second, own, TILE), jnp.bfloat16),
            pltpu.VMEM((second, own, TILE), jnp.bfloat16),
            pltpu.VMEM((second - 1, own, TILE), jnp.bfloat16),
            pltpu.SemaphoreType.DMA((2, 2 * (nr + nc))),
        ]
    return kinds


def exchange_kernel(grid_ref, ext_ref, density_ref, pots_ref, *scratch):
    greet()
    parts = []
    for h, order in enumerate(ORDERS):
        bufs = scratch[6 * h : 6 * h + 6]
        parts.append(Exchange(order, grid_ref.at[h], pots_ref.at[h], bufs[:5], bufs[5]))
    for part in parts:
        part.start1()
    for part in parts:
        part.start2()
    for part in parts:
        part.start3()
    for h, part in enumerate(parts):
        density = part.finish()
        columns = pl.ds(h * TILE, TILE)
        density_ref[:, columns] = density
        part.start4(ext_ref[:, columns] + 0.5 * density)
    for part in parts:
        part.start5()
    for part in parts:
        part.start6()
    for part in parts:
        part.wait()


def local(
    density_blocks, block_owner, block_plane, block_segment, block_kinds, basis, ext_potential
):
    count = density_blocks.shape[0]
    kinds, width, cells = basis.shape
    zplanes = ext_potential.shape[0]
    segs = ext_potential.shape[1] // SEGW
    nz = zplanes * lax.axis_size(AXES)
    first = block_owner[:, 0] * zplanes + block_plane
    planes = (first[None, :] + jnp.arange(CZB, dtype=jnp.int32)[:, None]) % nz
    rowid = (planes * segs + block_segment[None, :]).reshape(-1)
    flat_basis = basis.reshape(kinds * width, cells)
    hot = block_kinds[:, 1][:, None] == jnp.arange(kinds, dtype=jnp.int32)[None, :]
    cubes = density_blocks.reshape(count, width, 1, width)
    wide = jnp.where(hot[:, None, :, None], cubes, jnp.zeros((), jnp.bfloat16))
    wide = wide.reshape(count * width, kinds * width)
    places = CZB * count

    grid = pl.pallas_call(
        functools.partial(deposit_kernel, width, count),
        out_shape=jax.ShapeDtypeStruct((SEGW // TILE, nz * segs, TILE), jnp.bfloat16),
        in_specs=[SMEM, VMEM, VMEM, VMEM],
        out_specs=VMEM,
        scratch_shapes=[pltpu.VMEM((places, SEGW), jnp.float32)],
        compiler_params=pltpu.CompilerParams(vmem_limit_bytes=50 << 20),
    )(block_kinds, rowid.reshape(1, places), wide, flat_basis)

    nr, nc, ns = (lax.axis_size(axis) for axis in AXES)
    own = zplanes * segs
    split_grid = (SEGW // TILE, nr, nc, ns, own, TILE)
    density, pots = pl.pallas_call(
        exchange_kernel,
        out_shape=(
            jax.ShapeDtypeStruct((own, SEGW), jnp.float32),
            jax.ShapeDtypeStruct(split_grid, jnp.bfloat16),
        ),
        in_specs=[VMEM, VMEM],
        out_specs=(VMEM, VMEM),
        scratch_shapes=exchange_scratch(nr, nc, ns, own),
        compiler_params=pltpu.CompilerParams(
            collective_id=0, has_side_effects=True, vmem_limit_bytes=50 << 20
        ),
    )(grid.reshape(split_grid), ext_potential.reshape(own, SEGW))
    pots = pots.reshape(SEGW // TILE, nz * segs, TILE)

    blocks = pl.pallas_call(
        functools.partial(integrate_kernel, width, count),
        out_shape=jax.ShapeDtypeStruct((count * width, width), jnp.bfloat16),
        in_specs=[SMEM, VMEM, VMEM, VMEM],
        out_specs=VMEM,
        scratch_shapes=[
            pltpu.VMEM((places, SEGW), jnp.float32),
            pltpu.VMEM((8 * width, cells), jnp.bfloat16),
        ],
        compiler_params=pltpu.CompilerParams(vmem_limit_bytes=50 << 20),
    )(block_kinds, rowid.reshape(places, 1), pots, flat_basis)
    return density.reshape(zplanes, -1), blocks.reshape(count, width * width)


def solution(mesh):
    split = P(AXES, None)
    return jax.shard_map(
        local,
        mesh=mesh,
        in_specs=(split, split, P(AXES), P(AXES), split, P(), split),
        out_specs=(split, split),
        check_vma=False,
    )
```

```python
import functools

import jax
import jax.numpy as jnp
from jax import lax
from jax.experimental import pallas as pl
from jax.experimental.pallas import tpu as pltpu
from jax.sharding import PartitionSpec as P

CZB = 8
SEGW = 512
TILE = 256
AXES = ("rows", "cols", "slab")
VMEM = pl.BlockSpec(memory_space=pltpu.VMEM)
MESH = pl.DeviceIdType.MESH
SMEM = pl.BlockSpec(memory_space=pltpu.SMEM)


def peers_of(axis):
    size = lax.axis_size(axis)
    me = lax.axis_index(axis)
    return [lax.rem(me + o, size) for o in range(1, size)]


def greet():
    barrier = pltpu.get_barrier_semaphore()
    total = 0
    for axis in AXES:
        for peer in peers_of(axis):
            pl.semaphore_signal(barrier, inc=1, device_id={axis: peer}, device_id_type=MESH)
            total += 1
    pl.semaphore_wait(barrier, total)


def send(axis, peer, src, dst, sems, at):
    copy = pltpu.make_async_remote_copy(
        src_ref=src,
        dst_ref=dst,
        send_sem=sems.at[0, at],
        recv_sem=sems.at[1, at],
        device_id={axis: peer},
        device_id_type=MESH,
    )
    copy.start()
    return copy


class Exchange:
    def __init__(self, order, grid, pots, bufs, sems):
        self.order, self.grid, self.pots, self.sems = order, grid, pots, sems
        self.got1, self.sum1, self.got2, self.sum2, self.got3 = bufs
        self.r, self.c, self.s = (lax.axis_index(axis) for axis in AXES)
        self.sizes = {axis: lax.axis_size(axis) for axis in AXES}
        self.used = 0

    def next_sem(self):
        self.used += 1
        return self.used - 1

    def start1(self):
        (peer,) = peers_of("slab")
        self.copies = [
            send("slab", peer, self.grid.at[:, :, peer], self.got1, self.sems, self.next_sem())
        ]

    def wait(self):
        for copy in self.copies:
            copy.wait()

    def start2(self):
        self.wait()
        nr, nc = self.sizes["rows"], self.sizes["cols"]

        def add(n, carry):
            r, c = n // nc, n % nc
            self.sum1[r, c] = (
                self.grid[r, c, self.s].astype(jnp.float32) + self.got1[r, c].astype(jnp.float32)
            ).astype(jnp.bfloat16)
            return carry

        lax.fori_loop(0, nr * nc, add, 0)
        axis = self.order[0]
        self.copies = []
        for o, peer in enumerate(peers_of(axis)):
            src = self.sum1.at[peer] if axis == "rows" else self.sum1.at[:, peer]
            self.copies.append(send(axis, peer, src, self.got2.at[o], self.sems, self.next_sem()))

    def start3(self):
        self.wait()
        first, axis = self.order

        def add(n, carry):
            mine = self.sum1[self.r, n] if first == "rows" else self.sum1[n, self.c]
            total = mine.astype(jnp.float32)
            for o in range(self.sizes[first] - 1):
                total = total + self.got2[o, n].astype(jnp.float32)
            self.sum2[n] = total.astype(jnp.bfloat16)
            return carry

        lax.fori_loop(0, self.sizes[axis], add, 0)
        self.copies = []
        for o, peer in enumerate(peers_of(axis)):
            self.copies.append(
                send(axis, peer, self.sum2.at[peer], self.got3.at[o], self.sems, self.next_sem())
            )

    def finish(self):
        self.wait()
        axis = self.order[1]
        total = self.sum2[self.r if axis == "rows" else self.c].astype(jnp.float32)
        for o in range(self.sizes[axis] - 1):
            total = total + self.got3[o].astype(jnp.float32)
        return total

    def start4(self, potential):
        self.pots[self.r, self.c, self.s] = potential.astype(jnp.bfloat16)
        axis = self.order[1]
        mine = self.pots.at[self.r, self.c, self.s]
        self.copies = [
            send(axis, peer, mine, mine, self.sems, self.next_sem()) for peer in peers_of(axis)
        ]

    def start5(self):
        self.wait()
        axis = self.order[0]
        if axis == "rows":
            mine = self.pots.at[self.r, :, self.s]
        else:
            mine = self.pots.at[:, self.c, self.s]
        self.copies = [
            send(axis, peer, mine, mine, self.sems, self.next_sem()) for peer in peers_of(axis)
        ]

    def start6(self):
        self.wait()
        (peer,) = peers_of("slab")
        mine = self.pots.at[:, :, self.s]
        self.copies = [send("slab", peer, mine, mine, self.sems, self.next_sem())]


ORDERS = (("cols", "rows"), ("rows", "cols"))


def exchange_scratch(nr, nc, ns, own):
    kinds = []
    for order in ORDERS:
        first, second = (nr, nc) if order[0] == "rows" else (nc, nr)
        kinds += [
            pltpu.VMEM((nr, nc, own, TILE), jnp.bfloat16),
            pltpu.VMEM((nr, nc, own, TILE), jnp.bfloat16),
            pltpu.VMEM((first - 1, second, own, TILE), jnp.bfloat16),
            pltpu.VMEM((second, own, TILE), jnp.bfloat16),
            pltpu.VMEM((second - 1, own, TILE), jnp.bfloat16),
            pltpu.SemaphoreType.DMA((2, 2 * (nr + nc))),
        ]
    return kinds


def fused_kernel(
    width,
    count,
    kinds_ref,
    row_ref,
    column_ref,
    blocks_ref,
    basis_ref,
    ext_ref,
    density_ref,
    out_ref,
    halves_ref,
    wide_ref,
    tiles_ref,
    grid_ref,
    pots_ref,
    weighted_ref,
    full_ref,
    *scratch,
):
    group = 8
    groups = count // group
    kinds = basis_ref.shape[0]
    nr, nc, ns, own = grid_ref.shape[1:5]
    places = tiles_ref.shape[0]

    for h in range(SEGW // TILE):
        for i in range(CZB):
            halves_ref[h, :, :, i * TILE : (i + 1) * TILE] = basis_ref[
                :, :, i * SEGW + h * TILE : i * SEGW + (h + 1) * TILE
            ]

    lane_kind = lax.broadcasted_iota(jnp.int32, (width, kinds * width), 1) // width
    for k in range(count):
        lines = blocks_ref[k * width : (k + 1) * width, :]
        copies = jnp.concatenate([lines] * kinds, axis=1)
        wide_ref[k * width : (k + 1) * width, :] = jnp.where(
            lane_kind == kinds_ref[k, 1], copies, jnp.zeros_like(copies)
        )

    def of_kind(h, kind, columns):
        return halves_ref[h, kind, :, columns]

    def deposit(h, first, last):
        def column_tile(i, carry):
            columns = pl.ds(pl.multiple_of(i * TILE, TILE), TILE)
            weights = halves_ref[h, :, :, columns].reshape(kinds * width, TILE)
            for g in range(groups):
                lhs = wide_ref[g * group * width : (g + 1) * group * width, :]
                half = jnp.dot(lhs, weights, preferred_element_type=jnp.float32)
                sums = []
                for b in range(group):
                    a = of_kind(h, kinds_ref[g * group + b, 0], columns)
                    product = a.astype(jnp.float32) * half[b * width : (b + 1) * width]
                    sums.append(jnp.sum(product, axis=0, keepdims=True))
                row = pl.multiple_of(i * count + g * group, group)
                tiles_ref[pl.ds(row, group), :] = jnp.concatenate(sums, axis=0)
            return carry

        lax.fori_loop(first, last, column_tile, 0)

    def place(h):
        tiles = tiles_ref[...].astype(jnp.bfloat16)

        def one(n, carry):
            r, c = n // nc, n % nc
            rows = lax.broadcasted_iota(jnp.int32, (ns * own, places), 0) + n * ns * own
            hot = jnp.where(row_ref[...] == rows, 1.0, 0.0).astype(jnp.bfloat16)
            placed = jnp.dot(hot, tiles, preferred_element_type=jnp.float32).astype(jnp.bfloat16)
            for s in range(ns):
                grid_ref[h, r, c, s] = placed[s * own : (s + 1) * own]
            return carry

        lax.fori_loop(0, nr * nc, one, 0)

    def gather(h):
        tiles_ref[...] = jnp.zeros_like(tiles_ref)

        def one(r, carry):
            rows = nc * ns * own
            values = pots_ref[h, r].reshape(rows, TILE)
            places_of = lax.broadcasted_iota(jnp.int32, (places, rows), 1) + r * rows
            hot = jnp.where(column_ref[...] == places_of, 1.0, 0.0).astype(jnp.bfloat16)
            tiles_ref[...] += jnp.dot(hot, values, preferred_element_type=jnp.float32)
            return carry

        lax.fori_loop(0, nr, one, 0)

    def integrate(h, first, last):
        def block_group(g, carry):
            for i in range(CZB):
                rows = pl.ds(pl.multiple_of(i * count + g * group, group), group)
                pots = tiles_ref[rows, :]
                columns = pl.ds(i * TILE, TILE)
                for b in range(group):
                    a = of_kind(h, kinds_ref[g * group + b, 0], columns)
                    row = jnp.broadcast_to(pots[b : b + 1], (width, TILE)).astype(jnp.bfloat16)
                    weighted_ref[b * width : (b + 1) * width, i * TILE : (i + 1) * TILE] = a * row
            full = lax.dot_general(
                weighted_ref[...],
                halves_ref[h].reshape(kinds * width, CZB * TILE),
                (((1,), (1,)), ((), ())),
                preferred_element_type=jnp.float32,
            )
            lines = pl.ds(pl.multiple_of(g * group * width, group * width), group * width)
            if h < SEGW // TILE - 1:
                if h > 0:
                    full = full + full_ref[lines, :]
                full_ref[lines, :] = full
                return carry
            full = full + full_ref[lines, :]
            for b in range(group):
                kind = kinds_ref[g * group + b, 1]
                mine = jnp.where(lane_kind == kind, full[b * width : (b + 1) * width], 0.0)
                picked = mine[:, :width]
                for k in range(1, kinds):
                    picked = picked + mine[:, k * width : (k + 1) * width]
                out_ref[pl.ds(pl.multiple_of((g * group + b) * width, width), width), :] = (
                    picked.astype(jnp.bfloat16)
                )
            return carry

        lax.fori_loop(first, last, block_group, 0)

    parts = []
    for h, order in enumerate(ORDERS):
        bufs = scratch[6 * h : 6 * h + 6]
        parts.append(Exchange(order, grid_ref.at[h], pots_ref.at[h], bufs[:5], bufs[5]))
    early, late = parts

    def settle(h):
        density = parts[h].finish()
        columns = pl.ds(h * TILE, TILE)
        density_ref[:, columns] = density
        parts[h].start4(ext_ref[:, columns] + 0.5 * density)

    deposit(0, 0, CZB)
    place(0)
    greet()
    early.start1()
    deposit(1, 0, 2)
    early.start2()
    deposit(1, 2, 6)
    early.start3()
    deposit(1, 6, CZB)
    place(1)
    late.start1()
    settle(0)
    late.start2()
    early.start5()
    late.start3()
    early.start6()
    settle(1)
    early.wait()
    gather(0)
    integrate(0, 0, groups // 2)
    late.start5()
    integrate(0, groups // 2, groups)
    late.start6()
    late.wait()
    gather(1)
    integrate(1, 0, groups)


def local(
    density_blocks, block_owner, block_plane, block_segment, block_kinds, basis, ext_potential
):
    count = density_blocks.shape[0]
    kinds, width, cells = basis.shape
    zplanes = ext_potential.shape[0]
    segs = ext_potential.shape[1] // SEGW
    nz = zplanes * lax.axis_size(AXES)
    first = block_owner[:, 0] * zplanes + block_plane
    planes = (first[None, :] + jnp.arange(CZB, dtype=jnp.int32)[:, None]) % nz
    rowid = (planes * segs + block_segment[None, :]).reshape(-1)
    places = CZB * count

    nr, nc, ns = (lax.axis_size(axis) for axis in AXES)
    own = zplanes * segs
    halves = SEGW // TILE
    density, blocks = pl.pallas_call(
        functools.partial(fused_kernel, width, count),
        out_shape=(
            jax.ShapeDtypeStruct((own, SEGW), jnp.float32),
            jax.ShapeDtypeStruct((count * width, width), jnp.bfloat16),
        ),
        in_specs=[SMEM, VMEM, VMEM, VMEM, VMEM, VMEM],
        out_specs=(VMEM, VMEM),
        scratch_shapes=[
            pltpu.VMEM((halves, kinds, width, cells // halves), jnp.bfloat16),
            pltpu.VMEM((count * width, kinds * width), jnp.bfloat16),
            pltpu.VMEM((places, TILE), jnp.float32),
            pltpu.VMEM((halves, nr, nc, ns, own, TILE), jnp.bfloat16),
            pltpu.VMEM((halves, nr, nc, ns, own, TILE), jnp.bfloat16),
            pltpu.VMEM((8 * width, cells // halves), jnp.bfloat16),
            pltpu.VMEM((count * width, kinds * width), jnp.float32),
            *exchange_scratch(nr, nc, ns, own),
        ],
        compiler_params=pltpu.CompilerParams(
            collective_id=0, has_side_effects=True, vmem_limit_bytes=60 << 20
        ),
    )(
        block_kinds,
        rowid.reshape(1, places),
        rowid.reshape(places, 1),
        density_blocks.reshape(count * width, width),
        basis,
        ext_potential.reshape(own, SEGW),
    )
    return density.reshape(zplanes, -1), blocks.reshape(count, width * width)


def solution(mesh):
    split = P(AXES, None)
    return jax.shard_map(
        local,
        mesh=mesh,
        in_specs=(split, split, P(AXES), P(AXES), split, P(), split),
        out_specs=(split, split),
        check_vma=False,
    )
```

```python
import functools

import jax
import jax.numpy as jnp
from jax import lax
from jax.experimental import pallas as pl
from jax.experimental.pallas import tpu as pltpu
from jax.sharding import PartitionSpec as P

CZB = 8
SEGW = 512
TILE = 256
AXES = ("rows", "cols", "slab")
VMEM = pl.BlockSpec(memory_space=pltpu.VMEM)
MESH = pl.DeviceIdType.MESH
SMEM = pl.BlockSpec(memory_space=pltpu.SMEM)


def peers_of(axis):
    size = lax.axis_size(axis)
    me = lax.axis_index(axis)
    return [lax.rem(me + o, size) for o in range(1, size)]


def greet():
    barrier = pltpu.get_barrier_semaphore()
    total = 0
    for axis in AXES:
        for peer in peers_of(axis):
            pl.semaphore_signal(barrier, inc=1, device_id={axis: peer}, device_id_type=MESH)
            total += 1
    pl.semaphore_wait(barrier, total)


class Exchange:
    def __init__(self, grid, pots, bufs):
        self.grid, self.pots = grid, pots
        self.got1, self.sum1, self.got2, self.sum2, self.got3, self.sems = bufs
        self.r, self.c, self.s = (lax.axis_index(axis) for axis in AXES)
        self.nr, self.nc = (lax.axis_size(axis) for axis in AXES[:2])
        (self.twin,) = peers_of("slab")
        self.used = 0

    def send(self, axis, peer, src, dst):
        copy = pltpu.make_async_remote_copy(
            src_ref=src,
            dst_ref=dst,
            send_sem=self.sems.at[0, self.used],
            recv_sem=self.sems.at[1, self.used],
            device_id={axis: peer},
            device_id_type=MESH,
        )
        copy.start()
        self.used += 1
        return copy

    def toward(self, piece):
        return lax.rem(self.r + 1 + piece, self.nr)

    def reduce_slab(self):
        self.slab = [
            self.send("slab", self.twin, self.grid.at[self.toward(p), :, self.twin], self.got1.at[p])
            for p in range(self.nr)
        ]
        self.cols, self.rows = [], []

    def reduce_cols(self, p):
        self.slab[p].wait()
        row = self.toward(p)
        for c in range(self.nc):
            self.sum1[p, c] = (
                self.grid[row, c, self.s].astype(jnp.float32) + self.got1[p, c].astype(jnp.float32)
            ).astype(jnp.bfloat16)
        self.cols.append(
            [
                self.send("cols", peer, self.sum1.at[p, peer], self.got2.at[p, o])
                for o, peer in enumerate(peers_of("cols"))
            ]
        )

    def reduce_rows(self, p):
        for copy in self.cols[p]:
            copy.wait()
        total = self.sum1[p, self.c].astype(jnp.float32)
        for o in range(self.nc - 1):
            total = total + self.got2[p, o].astype(jnp.float32)
        self.sum2[p] = total.astype(jnp.bfloat16)
        if p < self.nr - 1:
            self.rows.append(
                self.send("rows", self.toward(p), self.sum2.at[p], self.got3.at[p])
            )

    def finish(self):
        for copy in self.rows:
            copy.wait()
        total = self.sum2[self.nr - 1].astype(jnp.float32)
        for p in range(self.nr - 1):
            total = total + self.got3[p].astype(jnp.float32)
        return total

    def spread_cols(self, row):
        mine = self.pots.at[row, self.c, self.s]
        self.cols.append([self.send("cols", peer, mine, mine) for peer in peers_of("cols")])

    def spread_rows(self, potential):
        self.pots[self.r, self.c, self.s] = potential.astype(jnp.bfloat16)
        mine = self.pots.at[self.r, self.c, self.s]
        self.rows = [
            self.send("rows", self.toward(p), mine, mine) for p in range(self.nr - 1)
        ]
        self.cols = []
        self.spread_cols(self.r)

    def source(self, piece):
        return lax.rem(self.r + self.nr - piece, self.nr)

    def pass_cols(self):
        for p in range(self.nr - 1):
            self.rows[p].wait()
            self.spread_cols(self.source(p + 1))

    def pass_slab(self):
        self.slab = []
        for p in range(self.nr):
            for copy in self.cols[p]:
                copy.wait()
            mine = self.pots.at[self.source(p), :, self.s]
            self.slab.append(self.send("slab", self.twin, mine, mine))

    def wait(self):
        for copy in self.slab:
            copy.wait()


def exchange_scratch(nr, nc, own):
    return [
        pltpu.VMEM((nr, nc, own, TILE), jnp.bfloat16),
        pltpu.VMEM((nr, nc, own, TILE), jnp.bfloat16),
        pltpu.VMEM((nr, nc - 1, own, TILE), jnp.bfloat16),
        pltpu.VMEM((nr, own, TILE), jnp.bfloat16),
        pltpu.VMEM((nr - 1, own, TILE), jnp.bfloat16),
        pltpu.SemaphoreType.DMA((2, 2 * (nr + nr * (nc - 1) + nr - 1))),
    ] * (SEGW // TILE)


def fused_kernel(
    width,
    count,
    codes_ref,
    blocks_ref,
    basis_ref,
    ext_ref,
    density_ref,
    out_ref,
    column_ref,
    halves_ref,
    wide_ref,
    tiles_ref,
    grid_ref,
    pots_ref,
    weighted_ref,
    full_ref,
    *scratch,
):
    group = 8
    groups = count // group
    kinds = basis_ref.shape[0]
    nr, nc, ns, own = grid_ref.shape[1:5]
    places = tiles_ref.shape[0]

    for h in range(SEGW // TILE):
        for i in range(CZB):
            halves_ref[h, :, :, i * TILE : (i + 1) * TILE] = basis_ref[
                :, :, i * SEGW + h * TILE : i * SEGW + (h + 1) * TILE
            ]

    total_rows = nr * nc * ns * own
    segs = own // density_ref.shape[0]
    block_of = lax.broadcasted_iota(jnp.int32, (count, 128), 0)
    lane_block = lax.broadcasted_iota(jnp.int32, (1, places), 1) % count
    base_column = jnp.zeros((count, 128), jnp.int32)
    base_row = jnp.zeros((1, places), jnp.int32)
    for k in range(count):
        base = lax.div(codes_ref[k], kinds * kinds)
        base_column = jnp.where(block_of == k, base, base_column)
        base_row = jnp.where(lane_block == k, base, base_row)
    for i in range(CZB):
        moved = base_column + i * segs
        column_ref[i * count : (i + 1) * count, :] = jnp.where(
            moved >= total_rows, moved - total_rows, moved
        )
    moved = base_row + lax.broadcasted_iota(jnp.int32, (1, places), 1) // count * segs
    row_of = jnp.where(moved >= total_rows, moved - total_rows, moved)

    lane_kind = lax.broadcasted_iota(jnp.int32, (width, kinds * width), 1) // width
    for k in range(count):
        lines = blocks_ref[k * width : (k + 1) * width, :]
        copies = jnp.concatenate([lines] * kinds, axis=1)
        wide_ref[k * width : (k + 1) * width, :] = jnp.where(
            lane_kind == lax.rem(codes_ref[k], kinds), copies, jnp.zeros_like(copies)
        )

    def of_kind(h, kind, columns):
        return halves_ref[h, kind, :, columns]

    def deposit(h, first, last):
        def column_tile(i, carry):
            columns = pl.ds(pl.multiple_of(i * TILE, TILE), TILE)
            weights = halves_ref[h, :, :, columns].reshape(kinds * width, TILE)
            for g in range(groups):
                lhs = wide_ref[g * group * width : (g + 1) * group * width, :]
                half = jnp.dot(lhs, weights, preferred_element_type=jnp.float32)
                sums = []
                for b in range(group):
                    a = of_kind(h, lax.rem(lax.div(codes_ref[g * group + b], kinds), kinds), columns)
                    product = a.astype(jnp.float32) * half[b * width : (b + 1) * width]
                    sums.append(jnp.sum(product, axis=0, keepdims=True))
                row = pl.multiple_of(i * count + g * group, group)
                tiles_ref[pl.ds(row, group), :] = jnp.concatenate(sums, axis=0)
            return carry

        if last > first:
            lax.fori_loop(first, last, column_tile, 0)

    def place(h):
        tiles = tiles_ref[...].astype(jnp.bfloat16)

        def one(n, carry):
            r, c = n // nc, n % nc
            rows = lax.broadcasted_iota(jnp.int32, (ns * own, places), 0) + n * ns * own
            hot = jnp.where(row_of == rows, 1.0, 0.0).astype(jnp.bfloat16)
            placed = jnp.dot(hot, tiles, preferred_element_type=jnp.float32).astype(jnp.bfloat16)
            for s in range(ns):
                grid_ref[h, r, c, s] = placed[s * own : (s + 1) * own]
            return carry

        lax.fori_loop(0, nr * nc, one, 0)

    def gather(h):
        tiles_ref[...] = jnp.zeros_like(tiles_ref)

        def one(r, carry):
            rows = nc * ns * own
            values = pots_ref[h, r].reshape(rows, TILE)
            column = jnp.concatenate([column_ref[...]] * (rows // 128), axis=1)
            places_of = lax.broadcasted_iota(jnp.int32, (places, rows), 1) + r * rows
            hot = jnp.where(column == places_of, 1.0, 0.0).astype(jnp.bfloat16)
            tiles_ref[...] += jnp.dot(hot, values, preferred_element_type=jnp.float32)
            return carry

        lax.fori_loop(0, nr, one, 0)

    def integrate(h, first, last):
        def block_group(g, carry):
            for i in range(CZB):
                rows = pl.ds(pl.multiple_of(i * count + g * group, group), group)
                pots = tiles_ref[rows, :]
                columns = pl.ds(i * TILE, TILE)
                for b in range(group):
                    a = of_kind(h, lax.rem(lax.div(codes_ref[g * group + b], kinds), kinds), columns)
                    row = jnp.broadcast_to(pots[b : b + 1], (width, TILE)).astype(jnp.bfloat16)
                    weighted_ref[b * width : (b + 1) * width, i * TILE : (i + 1) * TILE] = a * row
            full = lax.dot_general(
                weighted_ref[...],
                halves_ref[h].reshape(kinds * width, CZB * TILE),
                (((1,), (1,)), ((), ())),
                preferred_element_type=jnp.float32,
            )
            lines = pl.ds(pl.multiple_of(g * group * width, group * width), group * width)
            if h < SEGW // TILE - 1:
                if h > 0:
                    full = full + full_ref[lines, :]
                full_ref[lines, :] = full
                return carry
            full = full + full_ref[lines, :]
            for b in range(group):
                kind = lax.rem(codes_ref[g * group + b], kinds)
                mine = jnp.where(lane_kind == kind, full[b * width : (b + 1) * width], 0.0)
                picked = mine[:, :width]
                for k in range(1, kinds):
                    picked = picked + mine[:, k * width : (k + 1) * width]
                out_ref[pl.ds(pl.multiple_of((g * group + b) * width, width), width), :] = (
                    picked.astype(jnp.bfloat16)
                )
            return carry

        lax.fori_loop(first, last, block_group, 0)

    parts = []
    for h in range(SEGW // TILE):
        bufs = scratch[6 * h : 6 * h + 6]
        parts.append(Exchange(grid_ref.at[h], pots_ref.at[h], bufs))
    early, late = parts

    def settle(h):
        density = parts[h].finish().reshape(own // segs, segs, TILE)
        potential = []
        for s in range(segs):
            columns = pl.ds(s * SEGW + h * TILE, TILE)
            density_ref[:, columns] = density[:, s]
            potential.append(ext_ref[:, columns] + 0.5 * density[:, s])
        parts[h].spread_rows(jnp.stack(potential, axis=1).reshape(own, TILE))

    deposit(0, 0, CZB)
    place(0)
    greet()
    early.reduce_slab()
    deposit(1, 0, 1)
    for p in range(nr):
        early.reduce_cols(p)
    deposit(1, 1, 3)
    done = 3
    for p in range(nr):
        early.reduce_rows(p)
        more = 3 + (p + 1) * (CZB - 3) // nr
        deposit(1, done, more)
        done = more
    place(1)
    late.reduce_slab()
    settle(0)
    for p in range(nr):
        late.reduce_cols(p)
    early.pass_cols()
    for p in range(nr):
        late.reduce_rows(p)
    early.pass_slab()
    settle(1)
    early.wait()
    gather(0)
    integrate(0, 0, groups // 4)
    late.pass_cols()
    integrate(0, groups // 4, 5 * groups // 8)
    late.pass_slab()
    integrate(0, 5 * groups // 8, groups)
    late.wait()
    gather(1)
    integrate(1, 0, groups)


def local(
    density_blocks, block_owner, block_plane, block_segment, block_kinds, basis, ext_potential
):
    count = density_blocks.shape[0]
    kinds, width, cells = basis.shape
    zplanes = ext_potential.shape[0]
    segs = ext_potential.shape[1] // SEGW
    first = (block_owner[:, 0] * zplanes + block_plane) * segs + block_segment
    codes = (first * kinds + block_kinds[:, 0]) * kinds + block_kinds[:, 1]
    places = CZB * count

    nr, nc, ns = (lax.axis_size(axis) for axis in AXES)
    own = zplanes * segs
    halves = SEGW // TILE
    density, blocks = pl.pallas_call(
        functools.partial(fused_kernel, width, count),
        out_shape=(
            jax.ShapeDtypeStruct(ext_potential.shape, jnp.float32),
            jax.ShapeDtypeStruct((count * width, width), jnp.bfloat16),
        ),
        in_specs=[SMEM, VMEM, VMEM, VMEM],
        out_specs=(VMEM, VMEM),
        scratch_shapes=[
            pltpu.VMEM((places, 128), jnp.int32),
            pltpu.VMEM((halves, kinds, width, cells // halves), jnp.bfloat16),
            pltpu.VMEM((count * width, kinds * width), jnp.bfloat16),
            pltpu.VMEM((places, TILE), jnp.float32),
            pltpu.VMEM((halves, nr, nc, ns, own, TILE), jnp.bfloat16),
            pltpu.VMEM((halves, nr, nc, ns, own, TILE), jnp.bfloat16),
            pltpu.VMEM((8 * width, cells // halves), jnp.bfloat16),
            pltpu.VMEM((count * width, kinds * width), jnp.float32),
            *exchange_scratch(nr, nc, own),
        ],
        compiler_params=pltpu.CompilerParams(
            collective_id=0, has_side_effects=True, vmem_limit_bytes=60 << 20
        ),
    )(
        codes,
        density_blocks.reshape(count * width, width),
        basis,
        ext_potential,
    )
    return density, blocks.reshape(count, width * width)


def solution(mesh):
    split = P(AXES, None)
    return jax.shard_map(
        local,
        mesh=mesh,
        in_specs=(split, split, P(AXES), P(AXES), split, P(), split),
        out_specs=(split, split),
        check_vma=False,
    )
```

```python
import functools

import jax
import jax.numpy as jnp
from jax import lax
from jax.experimental import pallas as pl
from jax.experimental.pallas import tpu as pltpu
from jax.sharding import PartitionSpec as P

CZB = 8
SEGW = 512
TILE = 256
AXES = ("rows", "cols", "slab")
VMEM = pl.BlockSpec(memory_space=pltpu.VMEM)
MESH = pl.DeviceIdType.MESH
SMEM = pl.BlockSpec(memory_space=pltpu.SMEM)


def peers_of(axis):
    size = lax.axis_size(axis)
    me = lax.axis_index(axis)
    return [lax.rem(me + o, size) for o in range(1, size)]


def greet():
    barrier = pltpu.get_barrier_semaphore()
    total = 0
    for axis in AXES:
        for peer in peers_of(axis):
            pl.semaphore_signal(barrier, inc=1, device_id={axis: peer}, device_id_type=MESH)
            total += 1
    pl.semaphore_wait(barrier, total)


class Exchange:
    def __init__(self, grid, pots, bufs):
        self.grid, self.pots = grid, pots
        self.got1, self.sum1, self.got2, self.sum2, self.got3, self.sems = bufs
        self.r, self.c, self.s = (lax.axis_index(axis) for axis in AXES)
        self.nr, self.nc = (lax.axis_size(axis) for axis in AXES[:2])
        (self.twin,) = peers_of("slab")
        self.used = 0

    def send(self, axis, peer, src, dst):
        copy = pltpu.make_async_remote_copy(
            src_ref=src,
            dst_ref=dst,
            send_sem=self.sems.at[0, self.used],
            recv_sem=self.sems.at[1, self.used],
            device_id={axis: peer},
            device_id_type=MESH,
        )
        copy.start()
        self.used += 1
        return copy

    def toward(self, piece):
        return lax.rem(self.r + 1 + piece, self.nr)

    def reduce_slab(self):
        self.slab = [
            self.send("slab", self.twin, self.grid.at[self.toward(p), :, self.twin], self.got1.at[p])
            for p in range(self.nr)
        ]
        self.cols, self.rows = [], []

    def reduce_cols(self, p):
        self.slab[p].wait()
        row = self.toward(p)
        for c in range(self.nc):
            self.sum1[p, c] = (
                self.grid[row, c, self.s].astype(jnp.float32) + self.got1[p, c].astype(jnp.float32)
            ).astype(jnp.bfloat16)
        self.cols.append(
            [
                self.send("cols", peer, self.sum1.at[p, peer], self.got2.at[p, o])
                for o, peer in enumerate(peers_of("cols"))
            ]
        )

    def reduce_rows(self, p):
        for copy in self.cols[p]:
            copy.wait()
        total = self.sum1[p, self.c].astype(jnp.float32)
        for o in range(self.nc - 1):
            total = total + self.got2[p, o].astype(jnp.float32)
        self.sum2[p] = total.astype(jnp.bfloat16)
        if p < self.nr - 1:
            self.rows.append(
                self.send("rows", self.toward(p), self.sum2.at[p], self.got3.at[p])
            )

    def finish(self):
        for copy in self.rows:
            copy.wait()
        total = self.sum2[self.nr - 1].astype(jnp.float32)
        for p in range(self.nr - 1):
            total = total + self.got3[p].astype(jnp.float32)
        return total

    def spread_cols(self, row):
        mine = self.pots.at[row, self.c, self.s]
        self.cols.append([self.send("cols", peer, mine, mine) for peer in peers_of("cols")])

    def spread_rows(self, potential):
        self.pots[self.r, self.c, self.s] = potential.astype(jnp.bfloat16)
        mine = self.pots.at[self.r, self.c, self.s]
        self.rows = [
            self.send("rows", self.toward(p), mine, mine) for p in range(self.nr - 1)
        ]
        self.cols = []
        self.spread_cols(self.r)

    def source(self, piece):
        return lax.rem(self.r + self.nr - piece, self.nr)

    def pass_cols(self):
        for p in range(self.nr - 1):
            self.rows[p].wait()
            self.spread_cols(self.source(p + 1))

    def pass_slab(self):
        self.slab = []
        for p in range(self.nr):
            for copy in self.cols[p]:
                copy.wait()
            mine = self.pots.at[self.source(p), :, self.s]
            self.slab.append(self.send("slab", self.twin, mine, mine))

    def wait(self):
        for copy in self.slab:
            copy.wait()


def exchange_scratch(nr, nc, own):
    return [
        pltpu.VMEM((nr, nc, own, TILE), jnp.bfloat16),
        pltpu.VMEM((nr, nc, own, TILE), jnp.bfloat16),
        pltpu.VMEM((nr, nc - 1, own, TILE), jnp.bfloat16),
        pltpu.VMEM((nr, own, TILE), jnp.bfloat16),
        pltpu.VMEM((nr - 1, own, TILE), jnp.bfloat16),
        pltpu.SemaphoreType.DMA((2, 2 * (nr + nr * (nc - 1) + nr - 1))),
    ] * (SEGW // TILE)


def fused_kernel(
    width,
    count,
    codes_ref,
    blocks_ref,
    basis_ref,
    ext_ref,
    density_ref,
    out_ref,
    column_ref,
    halves_ref,
    wide_ref,
    tiles_ref,
    grid_ref,
    pots_ref,
    even_ref,
    odd_ref,
    turned_ref,
    full_ref,
    *scratch,
):
    group = 8
    groups = count // group
    kinds = basis_ref.shape[0]
    nr, nc, ns, own = grid_ref.shape[1:5]
    places = tiles_ref.shape[0]

    for h in range(SEGW // TILE):
        for i in range(CZB):
            halves_ref[h, :, :, i * TILE : (i + 1) * TILE] = basis_ref[
                :, :, i * SEGW + h * TILE : i * SEGW + (h + 1) * TILE
            ]

    total_rows = nr * nc * ns * own
    segs = own // density_ref.shape[0]
    block_of = lax.broadcasted_iota(jnp.int32, (count, 128), 0)
    lane_block = lax.broadcasted_iota(jnp.int32, (1, places), 1) % count
    base_column = jnp.zeros((count, 128), jnp.int32)
    base_row = jnp.zeros((1, places), jnp.int32)
    for k in range(count):
        base = lax.div(codes_ref[k], kinds * kinds)
        base_column = jnp.where(block_of == k, base, base_column)
        base_row = jnp.where(lane_block == k, base, base_row)
    for i in range(CZB):
        moved = base_column + i * segs
        column_ref[i * count : (i + 1) * count, :] = jnp.where(
            moved >= total_rows, moved - total_rows, moved
        )
    moved = base_row + lax.broadcasted_iota(jnp.int32, (1, places), 1) // count * segs
    row_of = jnp.where(moved >= total_rows, moved - total_rows, moved)

    lane_kind = lax.broadcasted_iota(jnp.int32, (width, kinds * width), 1) // width
    for k in range(count):
        lines = blocks_ref[k * width : (k + 1) * width, :]
        copies = jnp.concatenate([lines] * kinds, axis=1)
        wide_ref[k * width : (k + 1) * width, :] = jnp.where(
            lane_kind == lax.rem(codes_ref[k], kinds), copies, jnp.zeros_like(copies)
        )

    def of_kind(h, kind, columns):
        return halves_ref[h, kind, :, columns]

    def deposit(h, first, last):
        def column_tile(i, carry):
            columns = pl.ds(pl.multiple_of(i * TILE, TILE), TILE)
            weights = halves_ref[h, :, :, columns].reshape(kinds * width, TILE)
            for g in range(groups):
                lhs = wide_ref[g * group * width : (g + 1) * group * width, :]
                half = jnp.dot(lhs, weights, preferred_element_type=jnp.float32)
                half = half.astype(jnp.bfloat16)
                sums = []
                for b in range(group):
                    a = of_kind(h, lax.rem(lax.div(codes_ref[g * group + b], kinds), kinds), columns)
                    product = a * half[b * width : (b + 1) * width]
                    parts16 = [product[n : n + 16] for n in range(0, width, 16)]
                    while len(parts16) > 1:
                        parts16 = [x + y for x, y in zip(parts16[::2], parts16[1::2])]
                    part = parts16[0]
                    sums.append(jnp.sum(part.astype(jnp.float32), axis=0, keepdims=True))
                row = pl.multiple_of(i * count + g * group, group)
                tiles_ref[pl.ds(row, group), :] = jnp.concatenate(sums, axis=0)
            return carry

        if last > first:
            lax.fori_loop(first, last, column_tile, 0)

    def place(h):
        tiles = tiles_ref[...].astype(jnp.bfloat16)

        def one(n, carry):
            r, c = n // nc, n % nc
            rows = lax.broadcasted_iota(jnp.int32, (ns * own, places), 0) + n * ns * own
            hot = jnp.where(row_of == rows, 1.0, 0.0).astype(jnp.bfloat16)
            placed = jnp.dot(hot, tiles, preferred_element_type=jnp.float32).astype(jnp.bfloat16)
            for s in range(ns):
                grid_ref[h, r, c, s] = placed[s * own : (s + 1) * own]
            return carry

        lax.fori_loop(0, nr * nc, one, 0)

    def gather(h):
        tiles_ref[...] = jnp.zeros_like(tiles_ref)

        def one(r, carry):
            rows = nc * ns * own
            values = pots_ref[h, r].reshape(rows, TILE)
            column = jnp.concatenate([column_ref[...]] * (rows // 128), axis=1)
            places_of = lax.broadcasted_iota(jnp.int32, (places, rows), 1) + r * rows
            hot = jnp.where(column == places_of, 1.0, 0.0).astype(jnp.bfloat16)
            tiles_ref[...] += jnp.dot(hot, values, preferred_element_type=jnp.float32)
            return carry

        lax.fori_loop(0, nr, one, 0)

    def turn(h):
        def one(i, carry):
            columns = pl.ds(pl.multiple_of(i * TILE, TILE), TILE)
            flat = halves_ref[h, :, :, columns].reshape(kinds * width, TILE)
            turned_ref[h, columns, :] = flat.T
            return carry

        lax.fori_loop(0, CZB, one, 0)

    def build(h, g, buffer):
        for i in range(CZB):
            rows = pl.ds(pl.multiple_of(i * count + g * group, group), group)
            pots = tiles_ref[rows, :]
            columns = pl.ds(i * TILE, TILE)
            for b in range(group):
                code = codes_ref[g * group + b]
                a = of_kind(h, lax.rem(lax.div(code, kinds), kinds), columns)
                row = jnp.broadcast_to(pots[b : b + 1], (16, TILE)).astype(jnp.bfloat16)
                row = jnp.concatenate([row] * (width // 16), axis=0)
                buffer[b * width : (b + 1) * width, i * TILE : (i + 1) * TILE] = a * row

    def multiply(h, g, buffer):
        full = jnp.dot(buffer[...], turned_ref[h], preferred_element_type=jnp.float32)
        lines = pl.ds(pl.multiple_of(g * group * width, group * width), group * width)
        if h > 0:
            full = full + full_ref[lines, :]
        if h < SEGW // TILE - 1:
            full_ref[lines, :] = full
            return
        for b in range(group):
            kind = lax.rem(codes_ref[g * group + b], kinds)
            mine = jnp.where(lane_kind == kind, full[b * width : (b + 1) * width], 0.0)
            picked = mine[:, :width]
            for k in range(1, kinds):
                picked = picked + mine[:, k * width : (k + 1) * width]
            out_ref[pl.ds(pl.multiple_of((g * group + b) * width, width), width), :] = (
                picked.astype(jnp.bfloat16)
            )

    def integrate(h, first, last):
        def pair(n, carry):
            g = 2 * n
            multiply(h, g, even_ref)
            build(h, g + 1, odd_ref)
            multiply(h, g + 1, odd_ref)
            build(h, jnp.minimum(g + 2, groups - 2), even_ref)
            return carry

        if first == 0:
            build(h, 0, even_ref)
        lax.fori_loop(first // 2, last // 2, pair, 0)

    parts = []
    for h in range(SEGW // TILE):
        bufs = scratch[6 * h : 6 * h + 6]
        parts.append(Exchange(grid_ref.at[h], pots_ref.at[h], bufs))
    early, late = parts

    def settle(h):
        density = parts[h].finish().reshape(own // segs, segs, TILE)
        potential = []
        for s in range(segs):
            columns = pl.ds(s * SEGW + h * TILE, TILE)
            density_ref[:, columns] = density[:, s]
            potential.append(ext_ref[:, columns] + 0.5 * density[:, s])
        parts[h].spread_rows(jnp.stack(potential, axis=1).reshape(own, TILE))

    deposit(0, 0, CZB)
    place(0)
    greet()
    early.reduce_slab()
    deposit(1, 0, 1)
    for p in range(nr):
        early.reduce_cols(p)
    deposit(1, 1, 3)
    done = 3
    for p in range(nr):
        early.reduce_rows(p)
        more = 3 + (p + 1) * (CZB - 3) // nr
        deposit(1, done, more)
        done = more
    place(1)
    late.reduce_slab()
    settle(0)
    for p in range(nr):
        late.reduce_cols(p)
    turn(0)
    turn(1)
    for p in range(nr):
        late.reduce_rows(p)
    early.pass_cols()
    settle(1)
    early.pass_slab()
    early.wait()
    gather(0)
    integrate(0, 0, groups // 4)
    late.pass_cols()
    integrate(0, groups // 4, 3 * groups // 4)
    late.pass_slab()
    integrate(0, 3 * groups // 4, groups)
    late.wait()
    gather(1)
    integrate(1, 0, groups)


def local(
    density_blocks, block_owner, block_plane, block_segment, block_kinds, basis, ext_potential
):
    count = density_blocks.shape[0]
    kinds, width, cells = basis.shape
    zplanes = ext_potential.shape[0]
    segs = ext_potential.shape[1] // SEGW
    first = (block_owner[:, 0] * zplanes + block_plane) * segs + block_segment
    codes = (first * kinds + block_kinds[:, 0]) * kinds + block_kinds[:, 1]
    places = CZB * count

    nr, nc, ns = (lax.axis_size(axis) for axis in AXES)
    own = zplanes * segs
    halves = SEGW // TILE
    density, blocks = pl.pallas_call(
        functools.partial(fused_kernel, width, count),
        out_shape=(
            jax.ShapeDtypeStruct(ext_potential.shape, jnp.float32),
            jax.ShapeDtypeStruct((count * width, width), jnp.bfloat16),
        ),
        in_specs=[SMEM, VMEM, VMEM, VMEM],
        out_specs=(VMEM, VMEM),
        scratch_shapes=[
            pltpu.VMEM((places, 128), jnp.int32),
            pltpu.VMEM((halves, kinds, width, cells // halves), jnp.bfloat16),
            pltpu.VMEM((count * width, kinds * width), jnp.bfloat16),
            pltpu.VMEM((places, TILE), jnp.float32),
            pltpu.VMEM((halves, nr, nc, ns, own, TILE), jnp.bfloat16),
            pltpu.VMEM((halves, nr, nc, ns, own, TILE), jnp.bfloat16),
            pltpu.VMEM((8 * width, cells // halves), jnp.bfloat16),
            pltpu.VMEM((8 * width, cells // halves), jnp.bfloat16),
            pltpu.VMEM((halves, cells // halves, kinds * width), jnp.bfloat16),
            pltpu.VMEM((count * width, kinds * width), jnp.float32),
            *exchange_scratch(nr, nc, own),
        ],
        compiler_params=pltpu.CompilerParams(
            collective_id=0, has_side_effects=True, vmem_limit_bytes=60 << 20
        ),
    )(
        codes,
        density_blocks.reshape(count * width, width),
        basis,
        ext_potential,
    )
    return density, blocks.reshape(count, width * width)


def solution(mesh):
    split = P(AXES, None)
    return jax.shard_map(
        local,
        mesh=mesh,
        in_specs=(split, split, P(AXES), P(AXES), split, P(), split),
        out_specs=(split, split),
        check_vma=False,
    )
```

```python
import functools

import jax
import jax.numpy as jnp
from jax import lax
from jax.experimental import pallas as pl
from jax.experimental.pallas import tpu as pltpu
from jax.sharding import PartitionSpec as P

CZB = 8
SEGW = 512
TILE = 256
AXES = ("rows", "cols", "slab")
VMEM = pl.BlockSpec(memory_space=pltpu.VMEM)
MESH = pl.DeviceIdType.MESH
SMEM = pl.BlockSpec(memory_space=pltpu.SMEM)


def peers_of(axis):
    size = lax.axis_size(axis)
    me = lax.axis_index(axis)
    return [lax.rem(me + o, size) for o in range(1, size)]


def greet():
    barrier = pltpu.get_barrier_semaphore()
    total = 0
    for axis in AXES:
        for peer in peers_of(axis):
            pl.semaphore_signal(barrier, inc=1, device_id={axis: peer}, device_id_type=MESH)
            total += 1
    pl.semaphore_wait(barrier, total)


class Exchange:
    def __init__(self, grid, pots, bufs):
        self.grid, self.pots = grid, pots
        self.got1, self.sum1, self.got2, self.sum2, self.got3, self.sems = bufs
        self.r, self.c, self.s = (lax.axis_index(axis) for axis in AXES)
        self.nr, self.nc = (lax.axis_size(axis) for axis in AXES[:2])
        (self.twin,) = peers_of("slab")
        self.used = 0

    def send(self, axis, peer, src, dst):
        copy = pltpu.make_async_remote_copy(
            src_ref=src,
            dst_ref=dst,
            send_sem=self.sems.at[0, self.used],
            recv_sem=self.sems.at[1, self.used],
            device_id={axis: peer},
            device_id_type=MESH,
        )
        copy.start()
        self.used += 1
        return copy

    def toward(self, piece):
        return lax.rem(self.r + 1 + piece, self.nr)

    def reduce_slab(self):
        self.slab = [
            self.send("slab", self.twin, self.grid.at[self.toward(p), :, self.twin], self.got1.at[p])
            for p in range(self.nr)
        ]
        self.cols, self.rows = [], []

    def reduce_cols(self, p):
        self.slab[p].wait()
        row = self.toward(p)
        for c in range(self.nc):
            self.sum1[p, c] = (
                self.grid[row, c, self.s].astype(jnp.float32) + self.got1[p, c].astype(jnp.float32)
            ).astype(jnp.bfloat16)
        self.cols.append(
            [
                self.send("cols", peer, self.sum1.at[p, peer], self.got2.at[p, o])
                for o, peer in enumerate(peers_of("cols"))
            ]
        )

    def reduce_rows(self, p):
        for copy in self.cols[p]:
            copy.wait()
        total = self.sum1[p, self.c].astype(jnp.float32)
        for o in range(self.nc - 1):
            total = total + self.got2[p, o].astype(jnp.float32)
        self.sum2[p] = total.astype(jnp.bfloat16)
        if p < self.nr - 1:
            self.rows.append(
                self.send("rows", self.toward(p), self.sum2.at[p], self.got3.at[p])
            )

    def finish(self):
        for copy in self.rows:
            copy.wait()
        total = self.sum2[self.nr - 1].astype(jnp.float32)
        for p in range(self.nr - 1):
            total = total + self.got3[p].astype(jnp.float32)
        return total

    def spread_cols(self, row):
        mine = self.pots.at[row, self.c, self.s]
        self.cols.append([self.send("cols", peer, mine, mine) for peer in peers_of("cols")])

    def spread_rows(self, potential):
        self.pots[self.r, self.c, self.s] = potential.astype(jnp.bfloat16)
        mine = self.pots.at[self.r, self.c, self.s]
        self.rows = [
            self.send("rows", self.toward(p), mine, mine) for p in range(self.nr - 1)
        ]
        self.cols = []
        self.spread_cols(self.r)

    def source(self, piece):
        return lax.rem(self.r + self.nr - piece, self.nr)

    def pass_cols(self):
        for p in range(self.nr - 1):
            self.rows[p].wait()
            self.spread_cols(self.source(p + 1))

    def pass_slab(self):
        self.slab = []
        for p in range(self.nr):
            for copy in self.cols[p]:
                copy.wait()
            mine = self.pots.at[self.source(p), :, self.s]
            self.slab.append(self.send("slab", self.twin, mine, mine))

    def wait(self):
        for copy in self.slab:
            copy.wait()


def exchange_scratch(nr, nc, own):
    return [
        pltpu.VMEM((nr, nc, own, TILE), jnp.bfloat16),
        pltpu.VMEM((nr, nc, own, TILE), jnp.bfloat16),
        pltpu.VMEM((nr, nc - 1, own, TILE), jnp.bfloat16),
        pltpu.VMEM((nr, own, TILE), jnp.bfloat16),
        pltpu.VMEM((nr - 1, own, TILE), jnp.bfloat16),
        pltpu.SemaphoreType.DMA((2, 2 * (nr + nr * (nc - 1) + nr - 1))),
    ] * (SEGW // TILE)


def fused_kernel(
    width,
    count,
    codes_ref,
    blocks_ref,
    basis_ref,
    ext_ref,
    density_ref,
    out_ref,
    column_ref,
    halves_ref,
    wide_ref,
    tiles_ref,
    grid_ref,
    pots_ref,
    even_ref,
    odd_ref,
    turned_ref,
    full_ref,
    *scratch,
):
    group = 8
    groups = count // group
    kinds = basis_ref.shape[0]
    nr, nc, ns, own = grid_ref.shape[1:5]
    places = tiles_ref.shape[0]

    for h in range(SEGW // TILE):
        for i in range(CZB):
            halves_ref[h, :, :, i * TILE : (i + 1) * TILE] = basis_ref[
                :, :, i * SEGW + h * TILE : i * SEGW + (h + 1) * TILE
            ]

    total_rows = nr * nc * ns * own
    segs = own // density_ref.shape[0]
    block_of = lax.broadcasted_iota(jnp.int32, (count, 128), 0)
    lane_block = lax.broadcasted_iota(jnp.int32, (1, places), 1) % count
    base_column = jnp.zeros((count, 128), jnp.int32)
    base_row = jnp.zeros((1, places), jnp.int32)
    for k in range(count):
        base = lax.div(codes_ref[k], kinds * kinds)
        base_column = jnp.where(block_of == k, base, base_column)
        base_row = jnp.where(lane_block == k, base, base_row)
    for i in range(CZB):
        moved = base_column + i * segs
        column_ref[i * count : (i + 1) * count, :] = jnp.where(
            moved >= total_rows, moved - total_rows, moved
        )
    moved = base_row + lax.broadcasted_iota(jnp.int32, (1, places), 1) // count * segs
    row_of = jnp.where(moved >= total_rows, moved - total_rows, moved)

    lane_kind = lax.broadcasted_iota(jnp.int32, (width, kinds * width), 1) // width
    for k in range(count):
        lines = blocks_ref[k * width : (k + 1) * width, :]
        copies = jnp.concatenate([lines] * kinds, axis=1)
        wide_ref[k * width : (k + 1) * width, :] = jnp.where(
            lane_kind == lax.rem(codes_ref[k], kinds), copies, jnp.zeros_like(copies)
        )

    def of_kind(h, kind, columns):
        return halves_ref[h, kind, :, columns]

    def deposit(h, first, last):
        def column_tile(i, carry):
            columns = pl.ds(pl.multiple_of(i * TILE, TILE), TILE)
            weights = halves_ref[h, :, :, columns].reshape(kinds * width, TILE)
            for g in range(groups):
                lhs = wide_ref[g * group * width : (g + 1) * group * width, :]
                half = jnp.dot(lhs, weights, preferred_element_type=jnp.float32)
                half = half.astype(jnp.bfloat16)
                sums = []
                for b in range(group):
                    a = of_kind(h, lax.rem(lax.div(codes_ref[g * group + b], kinds), kinds), columns)
                    product = a * half[b * width : (b + 1) * width]
                    parts16 = [product[n : n + 16] for n in range(0, width, 16)]
                    while len(parts16) > 1:
                        parts16 = [x + y for x, y in zip(parts16[::2], parts16[1::2])]
                    part = parts16[0]
                    sums.append(jnp.sum(part.astype(jnp.float32), axis=0, keepdims=True))
                row = pl.multiple_of(i * count + g * group, group)
                tiles_ref[pl.ds(row, group), :] = jnp.concatenate(sums, axis=0)
            return carry

        if last > first:
            lax.fori_loop(first, last, column_tile, 0)

    def place(h):
        tiles = tiles_ref[...].astype(jnp.bfloat16)

        def one(n, carry):
            r, c = n // nc, n % nc
            rows = lax.broadcasted_iota(jnp.int32, (ns * own, places), 0) + n * ns * own
            hot = jnp.where(row_of == rows, 1.0, 0.0).astype(jnp.bfloat16)
            placed = jnp.dot(hot, tiles, preferred_element_type=jnp.float32).astype(jnp.bfloat16)
            for s in range(ns):
                grid_ref[h, r, c, s] = placed[s * own : (s + 1) * own]
            return carry

        lax.fori_loop(0, nr * nc, one, 0)

    def gather(h):
        tiles_ref[...] = jnp.zeros_like(tiles_ref)

        def one(r, carry):
            rows = nc * ns * own
            values = pots_ref[h, r].reshape(rows, TILE)
            column = jnp.concatenate([column_ref[...]] * (rows // 128), axis=1)
            places_of = lax.broadcasted_iota(jnp.int32, (places, rows), 1) + r * rows
            hot = jnp.where(column == places_of, 1.0, 0.0).astype(jnp.bfloat16)
            tiles_ref[...] += jnp.dot(hot, values, preferred_element_type=jnp.float32)
            return carry

        lax.fori_loop(0, nr, one, 0)

    def turn(h):
        def one(i, carry):
            columns = pl.ds(pl.multiple_of(i * TILE, TILE), TILE)
            flat = halves_ref[h, :, :, columns].reshape(kinds * width, TILE)
            turned_ref[h, columns, :] = flat.T
            return carry

        lax.fori_loop(0, CZB, one, 0)

    def build(h, g, buffer):
        for i in range(CZB):
            rows = pl.ds(pl.multiple_of(i * count + g * group, group), group)
            pots = tiles_ref[rows, :]
            columns = pl.ds(i * TILE, TILE)
            for b in range(group):
                code = codes_ref[g * group + b]
                a = of_kind(h, lax.rem(lax.div(code, kinds), kinds), columns)
                row = jnp.broadcast_to(pots[b : b + 1], (16, TILE)).astype(jnp.bfloat16)
                row = jnp.concatenate([row] * (width // 16), axis=0)
                buffer[b * width : (b + 1) * width, i * TILE : (i + 1) * TILE] = a * row

    def multiply(h, g, buffer):
        full = jnp.dot(buffer[...], turned_ref[h], preferred_element_type=jnp.float32)
        lines = pl.ds(pl.multiple_of(g * group * width, group * width), group * width)
        if h > 0:
            full = full + full_ref[lines, :]
        if h < SEGW // TILE - 1:
            full_ref[lines, :] = full
            return
        for b in range(group):
            kind = lax.rem(codes_ref[g * group + b], kinds)
            mine = jnp.where(lane_kind == kind, full[b * width : (b + 1) * width], 0.0)
            picked = mine[:, :width]
            for k in range(1, kinds):
                picked = picked + mine[:, k * width : (k + 1) * width]
            out_ref[pl.ds(pl.multiple_of((g * group + b) * width, width), width), :] = (
                picked.astype(jnp.bfloat16)
            )

    def integrate(h, first, last):
        def pair(n, carry):
            g = 2 * n
            multiply(h, g, even_ref)
            build(h, g + 1, odd_ref)
            multiply(h, g + 1, odd_ref)
            build(h, jnp.minimum(g + 2, groups - 2), even_ref)
            return carry

        if first == 0:
            build(h, 0, even_ref)
        lax.fori_loop(first // 2, last // 2, pair, 0)

    parts = []
    for h in range(SEGW // TILE):
        bufs = scratch[6 * h : 6 * h + 6]
        parts.append(Exchange(grid_ref.at[h], pots_ref.at[h], bufs))
    early, late = parts

    def settle(h):
        density = parts[h].finish().reshape(own // segs, segs, TILE)
        potential = []
        for s in range(segs):
            columns = pl.ds(s * SEGW + h * TILE, TILE)
            density_ref[:, columns] = density[:, s]
            potential.append(ext_ref[:, columns] + 0.5 * density[:, s])
        parts[h].spread_rows(jnp.stack(potential, axis=1).reshape(own, TILE))

    deposit(0, 0, CZB)
    place(0)
    greet()
    early.reduce_slab()
    deposit(1, 0, 1)
    for p in range(nr):
        early.reduce_cols(p)
    deposit(1, 1, 3)
    done = 3
    for p in range(nr):
        early.reduce_rows(p)
        more = 3 + (p + 1) * (CZB - 3) // nr
        deposit(1, done, more)
        done = more
    place(1)
    late.reduce_slab()
    settle(0)
    for p in range(nr):
        late.reduce_cols(p)
    early.pass_cols()
    turn(0)
    turn(1)
    for p in range(nr):
        late.reduce_rows(p)
    early.pass_slab()
    settle(1)
    early.wait()
    gather(0)
    integrate(0, 0, groups // 4)
    late.pass_cols()
    integrate(0, groups // 4, 3 * groups // 4)
    late.pass_slab()
    integrate(0, 3 * groups // 4, groups)
    late.wait()
    gather(1)
    integrate(1, 0, groups)


def local(
    density_blocks, block_owner, block_plane, block_segment, block_kinds, basis, ext_potential
):
    count = density_blocks.shape[0]
    kinds, width, cells = basis.shape
    zplanes = ext_potential.shape[0]
    segs = ext_potential.shape[1] // SEGW
    first = (block_owner[:, 0] * zplanes + block_plane) * segs + block_segment
    codes = (first * kinds + block_kinds[:, 0]) * kinds + block_kinds[:, 1]
    places = CZB * count

    nr, nc, ns = (lax.axis_size(axis) for axis in AXES)
    own = zplanes * segs
    halves = SEGW // TILE
    density, blocks = pl.pallas_call(
        functools.partial(fused_kernel, width, count),
        out_shape=(
            jax.ShapeDtypeStruct(ext_potential.shape, jnp.float32),
            jax.ShapeDtypeStruct((count * width, width), jnp.bfloat16),
        ),
        in_specs=[SMEM, VMEM, VMEM, VMEM],
        out_specs=(VMEM, VMEM),
        scratch_shapes=[
            pltpu.VMEM((places, 128), jnp.int32),
            pltpu.VMEM((halves, kinds, width, cells // halves), jnp.bfloat16),
            pltpu.VMEM((count * width, kinds * width), jnp.bfloat16),
            pltpu.VMEM((places, TILE), jnp.float32),
            pltpu.VMEM((halves, nr, nc, ns, own, TILE), jnp.bfloat16),
            pltpu.VMEM((halves, nr, nc, ns, own, TILE), jnp.bfloat16),
            pltpu.VMEM((8 * width, cells // halves), jnp.bfloat16),
            pltpu.VMEM((8 * width, cells // halves), jnp.bfloat16),
            pltpu.VMEM((halves, cells // halves, kinds * width), jnp.bfloat16),
            pltpu.VMEM((count * width, kinds * width), jnp.float32),
            *exchange_scratch(nr, nc, own),
        ],
        compiler_params=pltpu.CompilerParams(
            collective_id=0, has_side_effects=True, vmem_limit_bytes=60 << 20
        ),
    )(
        codes,
        density_blocks.reshape(count * width, width),
        basis,
        ext_potential,
    )
    return density, blocks.reshape(count, width * width)


def solution(mesh):
    split = P(AXES, None)
    return jax.shard_map(
        local,
        mesh=mesh,
        in_specs=(split, split, P(AXES), P(AXES), split, P(), split),
        out_specs=(split, split),
        check_vma=False,
    )
```
